256 devices in a mesh: ctx: 64 (over z, x, core), head: 4 (over y).
Axes of the slice: x: 4, y: 4, z: 8, core: 2. Of those that a mesh axis runs over, the one named last changes fastest.
Arguments:
- queries: bfloat16 [49152, 4096], P('ctx', 'head'), may hold values from -20 to 20
- keys: bfloat16 [49152, 4096], P('ctx', 'head'), may hold values from -6 to 6
- values: bfloat16 [49152, 4096], P('ctx', 'head'), may hold values from -64 to 64
- cotangent: bfloat16 [49152, 4096], P('ctx', 'head'), may hold values from -6 to 6
- state_in: float32 [32, 128, 128], P('head'), may hold values from -96 to 96
Outputs:
- output: bfloat16 [49152, 4096], P('ctx', 'head')
- grad_queries: bfloat16 [49152, 4096], P('ctx', 'head')
- grad_keys: bfloat16 [49152, 4096], P('ctx', 'head')
- grad_values: bfloat16 [49152, 4096], P('ctx', 'head')
The draws below stay inside these ranges and needn't reach their ends.
All inputs are finite; a program needn't handle non-finite values.
Results may differ from the reference program's by a relative error of at most 0.0058.
Values sent between devices are 32-bit elements; how exact they have to be, the bound alone decides.
A program may use at most 128 MiB of HBM per device.

```python
import math
import jax
import jax.numpy as jnp
from jax import lax

HEADS = 32
DH = 128
TOK_DEV = 768
SEQ = 49152


def draw_queries(key, part):
    entry_key, row_key = jax.random.split(jax.random.fold_in(key, 11), 2)
    feat_width = HEADS * DH
    row_scale = jnp.exp(jax.random.uniform(row_key, (SEQ, 1), jnp.float32, math.log(0.3), math.log(3.0)))
    entries = jax.random.normal(entry_key, (SEQ, feat_width), jnp.float32)
    return jnp.clip(entries * row_scale, -20.0, 20.0).astype(jnp.bfloat16)


def draw_values(key, part):
    entry_key, column_key = jax.random.split(jax.random.fold_in(key, 23), 2)
    feat_width = HEADS * DH
    head_number = (jnp.arange(feat_width) // DH).astype(jnp.float32)
    column_scale = 3.0 ** (head_number / (HEADS - 1)) * jnp.exp(jax.random.uniform(column_key, (feat_width,), jnp.float32, 0.0, math.log(3.5)))
    entries = jax.random.normal(entry_key, (SEQ, feat_width), jnp.float32)
    return jnp.clip(entries * column_scale[None, :], -64.0, 64.0).astype(jnp.bfloat16)


def block_levels(key, shape, pieces, least, largest):
    factor_of = 1.0
    for dim, parts in pieces:
        draws = jax.random.uniform(jax.random.fold_in(jax.random.fold_in(key, 6), dim), (parts,), jnp.float32, least / len(pieces), largest / len(pieces))
        factor_of = factor_of * jnp.repeat(jnp.exp(draws), shape[dim] // parts).reshape((-1,) + (1,) * (len(shape) - 1 - dim))
    return factor_of


def gaussian(rng, dims, spread, most, cuts=(), held_as=jnp.bfloat16):
    result = jax.random.normal(rng, dims, jnp.float32) * spread
    if len(cuts) > 0:
        result = block_levels(rng, dims, cuts, -0.22, 0.18) * result
    return jnp.clip(result, min=-most, max=most).astype(held_as)


def setup_inputs(seed: int = 0) -> dict:
    key_list = jax.random.split(jax.random.key(seed), 6)
    queries = draw_queries(jax.random.fold_in(key_list[5], 71), 0)
    keys = gaussian(key_list[1], (SEQ, HEADS * DH), 1.0, 6.0, ((0, 64), (1, 4)))
    values = draw_values(jax.random.fold_in(key_list[5], 71), 0)
    cotangent = gaussian(key_list[3], (SEQ, HEADS * DH), 1.0, 6.0, ((0, 64), (1, 4)))
    state_in = gaussian(key_list[4], (HEADS, DH, DH), 16.0, 96.0, ((0, 4),), jnp.float32)
    return dict(queries=queries, keys=keys, values=values, cotangent=cotangent, state_in=state_in)


def masked_product(left, right, causal_mask):
    scores = jnp.einsum('thi,shi->hts', left.astype(jnp.float32), right.astype(jnp.float32))
    return jnp.where(causal_mask[None], scores, 0.0).astype(jnp.bfloat16)

def reference(queries, keys, values, cotangent, state_in):
    seq_len = queries.shape[0]
    blocks = seq_len // TOK_DEV
    feat_count = HEADS * DH

    def split_blocks(array):
        return array.reshape(blocks, TOK_DEV, HEADS, DH)
    positions = jnp.arange(TOK_DEV)
    causal_mask = positions[:, None] >= positions[None, :]

    def forward_block(state_now, inputs):
        query_heads, key_heads, value_heads = inputs
        state_low = state_now.astype(jnp.bfloat16)
        scores = masked_product(query_heads, key_heads, causal_mask)
        attention = jnp.einsum('hts,she->the', scores.astype(jnp.float32), value_heads.astype(jnp.float32))
        attention = attention + jnp.einsum('thi,hie->the', query_heads.astype(jnp.float32), state_low.astype(jnp.float32))
        kv_block = jnp.einsum('shi,she->hie', key_heads.astype(jnp.float32), value_heads.astype(jnp.float32))
        return (state_now + kv_block, (attention, state_low))
    _, (attention, state_list) = lax.scan(forward_block, state_in, (split_blocks(queries), split_blocks(keys), split_blocks(values)))
    attention = attention.reshape(seq_len, feat_count)
    grad_float = cotangent.astype(jnp.float32)
    inverse_rms = lax.rsqrt(lax.optimization_barrier(jnp.sum(attention * attention, axis=1)) / feat_count + 1e-06)
    cross_sum = lax.optimization_barrier(jnp.sum(grad_float * attention, axis=1))
    output = (attention * inverse_rms[:, None]).astype(jnp.bfloat16)
    grad_attention = (inverse_rms[:, None] * grad_float - attention * (inverse_rms ** 3 * cross_sum / feat_count)[:, None]).astype(jnp.bfloat16)

    def backward_block(suffix_now, inputs):
        query_heads, key_heads, value_heads, grad_heads, state_low = inputs
        suffix_low = suffix_now.astype(jnp.bfloat16)
        query_float = query_heads.astype(jnp.float32)
        key_float = key_heads.astype(jnp.float32)
        value_float = value_heads.astype(jnp.float32)
        grad_f = grad_heads.astype(jnp.float32)
        scores = masked_product(query_heads, key_heads, causal_mask).astype(jnp.float32)
        grad_scores = masked_product(grad_heads, value_heads, causal_mask).astype(jnp.float32)
        grad_query = jnp.einsum('hts,shi->thi', grad_scores, key_float) + jnp.einsum('the,hie->thi', grad_f, state_low.astype(jnp.float32))
        grad_key = jnp.einsum('hts,thi->shi', grad_scores, query_float) + jnp.einsum('she,hie->shi', value_float, suffix_low.astype(jnp.float32))
        grad_value = jnp.einsum('hts,the->she', scores, grad_f) + jnp.einsum('shi,hie->she', key_float, suffix_low.astype(jnp.float32))
        qd_block = jnp.einsum('thi,the->hie', query_float, grad_f)
        return (suffix_now + qd_block, (grad_query.astype(jnp.bfloat16), grad_key.astype(jnp.bfloat16), grad_value.astype(jnp.bfloat16)))
    zero_state = jnp.zeros((HEADS, DH, DH), jnp.float32)
    _, (grad_query, grad_key, grad_value) = lax.scan(backward_block, zero_state, (split_blocks(queries), split_blocks(keys), split_blocks(values), split_blocks(grad_attention), state_list), reverse=True)
    return (output, grad_query.reshape(seq_len, feat_count), grad_key.reshape(seq_len, feat_count), grad_value.reshape(seq_len, feat_count))
```

```python
import jax
import jax.numpy as jnp
from jax import lax
from jax.experimental import pallas as pl
from jax.experimental.pallas import tpu as pltpu
from jax.sharding import PartitionSpec as P

HEADS = 32
DH = 128
TOK = 768
HERE = 8
HALF = 4
FEAT = HERE * DH
XS, YS, ZS = 4, 4, 8
SL = DH // ZS
BLK = 256
NBLK = TOK // BLK
F32 = jnp.float32
BF16 = jnp.bfloat16

NN = (((1,), (0,)), ((), ()))
NT = (((1,), (1,)), ((), ()))
TN = (((0,), (0,)), ((), ()))


def mm(a, b, dims):
    return lax.dot_general(a, b, dims, preferred_element_type=F32)


def cols(h):
    return pl.ds(pl.multiple_of(h * DH, DH), DH)


def send(src, dst, ssem, rsem, target):
    return pltpu.make_async_remote_copy(
        src_ref=src,
        dst_ref=dst,
        send_sem=ssem,
        recv_sem=rsem,
        device_id=target,
        device_id_type=pl.DeviceIdType.MESH,
    )


def main_kernel(
    q_hbm, k_hbm, v_hbm, c_hbm, s_hbm,
    out, gq, gkp, gvp, k, v, sfx,
    q, c, s0, sc, dsb, att, d, invb, wb, low, st,
    kv, cr, cs, xr, tt, zt, zp, zr, xp, pr, fs, fr,
    load_sem, cs_sem, cr_sem, xs_sem, xr_sem, zs_sem, zr_sem, ys_sem, yr_sem,
):
    ci = lax.axis_index("ctx")
    y = lax.axis_index("head")
    z = ci // (2 * XS)
    x = (ci // 2) % XS
    core = ci % 2

    def dev(zz, xx, cc, yy):
        return ((zz * XS + xx) * 2 + cc, yy)

    partner = dev(z, x, 1 - core, y)
    x_devs = [dev(z, (x + i) % XS, core, y) for i in range(1, XS)]
    z_devs = [dev((z + i) % ZS, x, core, y) for i in range(1, ZS)]
    y_devs = [dev(z, x, core, (y + i) % YS) for i in range(1, YS)]
    peers = [partner] + x_devs + z_devs + y_devs

    def half_cols(cc):
        return pl.ds(pl.multiple_of(cc * (HALF * DH), HALF * DH), HALF * DH)

    loads = []
    for n, cc in enumerate((1 - core, core)):
        for m, (src, dst) in enumerate(((k_hbm, k), (v_hbm, v))):
            loads.append(
                pltpu.make_async_copy(
                    src.at[:, half_cols(cc)], dst.at[:, half_cols(cc)], load_sem.at[2 * n + m]
                )
            )
    loads.append(pltpu.make_async_copy(q_hbm, q, load_sem.at[4]))
    loads.append(pltpu.make_async_copy(c_hbm, c, load_sem.at[5]))
    loads.append(
        pltpu.make_async_copy(
            s_hbm.at[core * HALF + x, pl.ds(pl.multiple_of(z * SL, SL), SL)], s0, load_sem.at[6]
        )
    )
    for copy in loads:
        copy.start()

    barrier = pltpu.get_barrier_semaphore()
    for peer in peers:
        pl.semaphore_signal(barrier, inc=1, device_id=peer, device_id_type=pl.DeviceIdType.MESH)

    def loop(lo, hi, body):
        def step(i, carry):
            body(i)
            return carry

        lax.fori_loop(lo, hi, step, 0)

    rows_i = lax.broadcasted_iota(jnp.int32, (BLK, BLK), 0)
    cols_i = lax.broadcasted_iota(jnp.int32, (BLK, BLK), 1)

    def scores_into(dst, left, right, h):
        for i in range(NBLK):
            rows = slice(i * BLK, (i + 1) * BLK)
            li = left[rows, cols(h)]
            for j in range(i + 1):
                s = mm(li, right[j * BLK:(j + 1) * BLK, cols(h)], NT)
                if i == j:
                    s = jnp.where(rows_i >= cols_i, s, 0.0)
                dst(rows, slice(j * BLK, (j + 1) * BLK), s.astype(BF16))

    def forward_unit(h):
        def put(rows, columns, val):
            sc[h, rows, columns] = val

        scores_into(put, q, k, h)
        for i in range(NBLK):
            rows = slice(i * BLK, (i + 1) * BLK)
            n = (i + 1) * BLK
            att[rows, cols(h)] = mm(sc[h, rows, 0:n], v[0:n, cols(h)], NN)

    def backward_unit(h):
        def put(rows, columns, val):
            dsb[rows, columns] = val

        scores_into(put, d, v, h)
        for i in range(NBLK):
            rows = slice(i * BLK, (i + 1) * BLK)
            n = (i + 1) * BLK
            g = mm(dsb[rows, 0:n], k[0:n, cols(h)], NN) + mm(d[rows, cols(h)], low[h], NT)
            gq[rows, cols(h)] = g.astype(BF16)
        qt = q[:, cols(h)].T
        dt = d[:, cols(h)].T
        for j in range(NBLK):
            columns = slice(j * BLK, (j + 1) * BLK)
            n = j * BLK
            gkp[columns, cols(h)] = mm(qt[:, n:], dsb[n:, columns], NN).T
            gvp[columns, cols(h)] = mm(dt[:, n:], sc[h, n:, columns], NN).T

    def scan(r, reverse, terms, state, work, done):
        own = core * HALF
        other = (1 - core) * HALF
        def term(j, base):
            kv[r, base + j] = terms(base + j).reshape(ZS, SL, DH)

        loop(0, HALF, lambda j: term(j, other))
        if r == 0:
            pl.semaphore_wait(barrier, len(peers))
        a = send(kv.at[r, pl.ds(other, HALF)], cr.at[r], cs_sem.at[r, 0], cr_sem.at[r, 0], partner)
        a.start()
        if r == 0:
            loads[2].wait()
            loads[3].wait()
        loop(0, HALF, lambda j: term(j, own))
        a.wait_recv()
        cs[r] = kv[r, pl.ds(own, HALF)] + cr[r]
        b = [
            send(cs.at[r, (x + i) % XS], xr.at[r, x], xs_sem.at[r, 0, i - 1], xr_sem.at[r, 0, i - 1], x_devs[i - 1])
            for i in (2, 1, 3)
        ]
        for copy in b:
            copy.start()
        xr[r, x] = cs[r, x]
        work(0)
        for copy in b:
            copy.wait_recv()
        tt[r] = xr[r, 0] + xr[r, 1] + xr[r, 2] + xr[r, 3]
        order = (4, 3, 5, 2, 6, 1, 7)
        e = [
            send(tt.at[r, (z + i) % ZS], zt.at[r, z], zs_sem.at[r, 0, i - 1], zr_sem.at[r, 0, i - 1], z_devs[i - 1])
            for i in order
        ]
        for copy in e:
            copy.start()
        zt[r, z] = tt[r, z]
        work(1)
        for copy in e:
            copy.wait_recv()
        total = state()
        for zz in range(ZS - 1, -1, -1) if reverse else range(ZS):
            zp[r, zz] = total
            total = total + zt[r, zz]
        f = [
            send(zp.at[r, (z + i) % ZS], zr.at[r, z], zs_sem.at[r, 1, i - 1], zr_sem.at[r, 1, i - 1], z_devs[i - 1])
            for i in order
        ]
        for copy in f:
            copy.start()
        zr[r, z] = zp[r, z]
        work(2)
        for copy in f:
            copy.wait_recv()
        total = zr[r]
        for xx in range(XS - 1, -1, -1) if reverse else range(XS):
            xp[r, xx] = total
            total = total + xr[r, xx]
        g = [
            send(xp.at[r, (x + i) % XS], pr.at[r, x], xs_sem.at[r, 1, i - 1], xr_sem.at[r, 1, i - 1], x_devs[i - 1])
            for i in (2, 1, 3)
        ]
        for copy in g:
            copy.start()
        pr[r, x] = xp[r, x]
        work(3)
        for copy in g:
            copy.wait_recv()
        later = core == (0 if reverse else 1)
        fs[r] = pr[r] + jnp.where(later, 0.0, kv[r, pl.ds(own, HALF)])
        o = send(fs.at[r], fr.at[r], cs_sem.at[r, 1], cr_sem.at[r, 1], partner)
        o.start()
        for j in range(HALF):
            done(own + j, (pr[r, j] + jnp.where(later, cr[r, j], 0.0)).reshape(DH, DH))
        o.wait_recv()
        for j in range(HALF):
            done(other + j, fr[r, j].reshape(DH, DH))
        for copy in [a] + b + e + f + g + [o]:
            copy.wait_send()

    loads[0].wait()
    loads[1].wait()

    def forward_term(h):
        return mm(k[:, cols(h)], v[:, cols(h)], TN)

    def forward_work(n):
        if n == 0:
            loads[4].wait()
        if n == 3:
            loads[5].wait()
        loop(2 * n, 2 * n + 2, forward_unit)

    def forward_state():
        loads[6].wait()
        return s0[...]

    def forward_done(h, val):
        low[h] = val.astype(BF16)

    scan(0, False, forward_term, forward_state, forward_work, forward_done)

    st[y] = jnp.zeros((8, TOK), F32)
    for i in range(NBLK):
        rows = slice(i * BLK, (i + 1) * BLK)
        squares = jnp.zeros((BLK, DH), F32)
        cross = jnp.zeros((BLK, DH), F32)
        for h in range(HERE):
            hc = slice(h * DH, (h + 1) * DH)
            a = att[rows, hc] + mm(q[rows, hc], low[h], NN)
            att[rows, hc] = a
            squares = squares + a * a
            cross = cross + a * c[rows, hc].astype(F32)
        st[y, 0:1, rows] = jnp.sum(squares.T, axis=0, keepdims=True)
        st[y, 1:2, rows] = jnp.sum(cross.T, axis=0, keepdims=True)
    stats = [
        send(st.at[y], st.at[y], ys_sem.at[i - 1], yr_sem.at[i - 1], y_devs[i - 1]) for i in (2, 1, 3)
    ]
    for copy in stats:
        copy.start()
    for copy in stats:
        copy.wait()
    total = st[0] + st[1] + st[2] + st[3]
    inv = lax.rsqrt(total[0:1] / (HEADS * DH) + 1e-06)
    weight = inv * inv * inv * total[1:2] / (HEADS * DH)
    invb[...] = jnp.broadcast_to(inv, (DH, TOK)).T
    wb[...] = jnp.broadcast_to(weight, (DH, TOK)).T

    def backward_term(h):
        a = att[:, cols(h)]
        out[:, cols(h)] = (a * invb[...]).astype(BF16)
        dh = (invb[...] * c[:, cols(h)].astype(F32) - a * wb[...]).astype(BF16)
        d[:, cols(h)] = dh
        return mm(q[:, cols(h)], dh, TN)

    def backward_work(n):
        loop(2 * n, 2 * n + 2, backward_unit)

    def backward_done(h, val):
        sfx[h] = val.astype(BF16)

    scan(1, True, backward_term, lambda: jnp.zeros((SL, DH), F32), backward_work, backward_done)


def last_kernel(out_in, gq_in, gkp, gvp, k, v, sfx, out, gq, gk, gv, gkb, gvb, sem):
    first = [
        pltpu.make_async_copy(out_in, out, sem.at[0, 0]),
        pltpu.make_async_copy(gq_in, gq, sem.at[0, 1]),
    ]
    for copy in first:
        copy.start()
    later = []
    for h in range(HERE):
        hc = slice(h * DH, (h + 1) * DH)
        gkb[:, hc] = (gkp[:, hc] + mm(v[:, hc], sfx[h], NT)).astype(BF16)
        gvb[:, hc] = (gvp[:, hc] + mm(k[:, hc], sfx[h], NN)).astype(BF16)
        if h % 2 == 1:
            two = slice((h - 1) * DH, (h + 1) * DH)
            for n, (src, dst) in enumerate(((gkb, gk), (gvb, gv))):
                copy = pltpu.make_async_copy(src.at[:, two], dst.at[:, two], sem.at[1 + h // 2, n])
                copy.start()
                later.append(copy)
    for copy in first + later:
        copy.wait()


def local(queries, keys, values, cotangent, state_in):
    hbm = pl.BlockSpec(memory_space=pltpu.HBM)
    vmem = pl.BlockSpec(memory_space=pltpu.VMEM)
    wide = (TOK, FEAT)
    mid = pl.pallas_call(
        main_kernel,
        name="scan_and_attention",
        out_shape=(
            pltpu.VMEM(wide, BF16),
            pltpu.VMEM(wide, BF16),
            pltpu.VMEM(wide, F32),
            pltpu.VMEM(wide, F32),
            pltpu.VMEM(wide, BF16),
            pltpu.VMEM(wide, BF16),
            pltpu.VMEM((HERE, DH, DH), BF16),
        ),
        in_specs=[hbm] * 5,
        out_specs=(vmem,) * 7,
        scratch_shapes=[
            pltpu.VMEM(wide, BF16),
            pltpu.VMEM(wide, BF16),
            pltpu.VMEM((SL, DH), F32),
            pltpu.VMEM((HERE, TOK, TOK), BF16),
            pltpu.VMEM((TOK, TOK), BF16),
            pltpu.VMEM(wide, F32),
            pltpu.VMEM(wide, BF16),
            pltpu.VMEM((TOK, DH), F32),
            pltpu.VMEM((TOK, DH), F32),
            pltpu.VMEM((HERE, DH, DH), BF16),
            pltpu.VMEM((YS, 8, TOK), F32),
            pltpu.VMEM((2, HERE, ZS, SL, DH), F32),
            pltpu.VMEM((2, HALF, ZS, SL, DH), F32),
            pltpu.VMEM((2, HALF, ZS, SL, DH), F32),
            pltpu.VMEM((2, XS, ZS, SL, DH), F32),
            pltpu.VMEM((2, ZS, SL, DH), F32),
            pltpu.VMEM((2, ZS, SL, DH), F32),
            pltpu.VMEM((2, ZS, SL, DH), F32),
            pltpu.VMEM((2, ZS, SL, DH), F32),
            pltpu.VMEM((2, XS, ZS, SL, DH), F32),
            pltpu.VMEM((2, XS, ZS, SL, DH), F32),
            pltpu.VMEM((2, HALF, ZS, SL, DH), F32),
            pltpu.VMEM((2, HALF, ZS, SL, DH), F32),
            pltpu.SemaphoreType.DMA((7,)),
            pltpu.SemaphoreType.DMA((2, 2)),
            pltpu.SemaphoreType.DMA((2, 2)),
            pltpu.SemaphoreType.DMA((2, 2, XS - 1)),
            pltpu.SemaphoreType.DMA((2, 2, XS - 1)),
            pltpu.SemaphoreType.DMA((2, 2, ZS - 1)),
            pltpu.SemaphoreType.DMA((2, 2, ZS - 1)),
            pltpu.SemaphoreType.DMA((YS - 1,)),
            pltpu.SemaphoreType.DMA((YS - 1,)),
        ],
        compiler_params=pltpu.CompilerParams(
            collective_id=0, has_side_effects=True, vmem_limit_bytes=40 * 2**20
        ),
    )(queries, keys, values, cotangent, state_in)
    return pl.pallas_call(
        last_kernel,
        name="add_states",
        out_shape=(jax.ShapeDtypeStruct(wide, BF16),) * 4,
        in_specs=[vmem] * 7,
        out_specs=(hbm,) * 4,
        scratch_shapes=[
            pltpu.VMEM(wide, BF16),
            pltpu.VMEM(wide, BF16),
            pltpu.SemaphoreType.DMA((5, 2)),
        ],
        compiler_params=pltpu.CompilerParams(vmem_limit_bytes=16 * 2**20),
    )(*mid)


def solution(mesh):
    wide = P("ctx", "head")
    return jax.shard_map(
        local,
        mesh=mesh,
        in_specs=(wide, wide, wide, wide, P("head", None, None)),
        out_specs=(wide, wide, wide, wide),
        check_vma=False,
    )
```

```python
import jax
import jax.numpy as jnp
from jax import lax
from jax.experimental import pallas as pl
from jax.experimental.pallas import tpu as pltpu
from jax.sharding import PartitionSpec as P

HEADS = 32
DH = 128
TOK = 768
HERE = 8
HALF = 4
FEAT = HERE * DH
XS, YS, ZS = 4, 4, 8
CHIPS = XS * ZS
CHUNKS = 2
PAIR = HALF // CHUNKS
SL = PAIR * DH // CHIPS
FORWARD_UNITS = (0, 6, 7, 8, 8)
BACKWARD_UNITS = (0, 4, 5, 7, 8)
BLK = 256
NBLK = TOK // BLK
F32 = jnp.float32
BF16 = jnp.bfloat16

NN = (((1,), (0,)), ((), ()))
NT = (((1,), (1,)), ((), ()))
TN = (((0,), (0,)), ((), ()))


def mm(a, b, dims):
    return lax.dot_general(a, b, dims, preferred_element_type=F32)


def cols(h):
    return pl.ds(pl.multiple_of(h * DH, DH), DH)


def send(src, dst, ssem, rsem, target):
    return pltpu.make_async_remote_copy(
        src_ref=src,
        dst_ref=dst,
        send_sem=ssem,
        recv_sem=rsem,
        device_id=target,
        device_id_type=pl.DeviceIdType.MESH,
    )


def main_kernel(
    q_hbm, k_hbm, v_hbm, c_hbm, s_hbm,
    out, gq, gkp, gvp, k, v, sfx,
    q, c, s0, sc, dsb, att, squares, cross, d, invb, wb, low, st,
    kv, cr, cs, got, back, pr, fs, fr,
    load_sem, cs_sem, cr_sem, fs_sem, fr_sem, ys_sem, yr_sem,
):
    ci = lax.axis_index("ctx")
    y = lax.axis_index("head")
    z = ci // (2 * XS)
    x = (ci // 2) % XS
    core = ci % 2
    chip = z * XS + x

    def dev(chip_index, cc, yy):
        return (chip_index * 2 + cc, yy)

    partner = dev(chip, 1 - core, y)
    others = []
    for dz in (4, 3, 5, 2, 6, 1, 7, 0):
        for dx in (2, 1, 3, 0):
            if dz or dx:
                others.append(((z + dz) % ZS) * XS + (x + dx) % XS)
    y_devs = [dev(chip, core, (y + i) % YS) for i in range(1, YS)]
    peers = [partner] + y_devs + [dev(o, core, y) for o in others]

    def head(half, ck, i=0):
        return half * HALF + ck * PAIR + i

    def pair_cols(half, ck):
        return pl.ds(pl.multiple_of(head(half, ck) * DH, PAIR * DH), PAIR * DH)

    loads = {}

    def load(name, src, dst):
        copy = pltpu.make_async_copy(src, dst, load_sem.at[len(loads)])
        copy.start()
        loads[name] = copy

    for ck in range(CHUNKS):
        for side, half in enumerate((1 - core, core)):
            part = pair_cols(half, ck)
            load(("k", ck, side), k_hbm.at[:, part], k.at[:, part])
            load(("v", ck, side), v_hbm.at[:, part], v.at[:, part])
    load("q", q_hbm, q)
    for ck in range(CHUNKS):
        rows = pl.ds(pl.multiple_of((chip % (CHIPS // PAIR)) * SL, SL), SL)
        load(("s", ck), s_hbm.at[head(core, ck) + chip // (CHIPS // PAIR), rows], s0.at[ck])
    load("c", c_hbm, c)

    barrier = pltpu.get_barrier_semaphore()
    for peer in peers:
        pl.semaphore_signal(barrier, inc=1, device_id=peer, device_id_type=pl.DeviceIdType.MESH)

    def loop(lo, hi, body):
        def step(i, carry):
            body(i)
            return carry

        if hi > lo:
            lax.fori_loop(lo, hi, step, 0)

    rows_i = lax.broadcasted_iota(jnp.int32, (BLK, BLK), 0)
    cols_i = lax.broadcasted_iota(jnp.int32, (BLK, BLK), 1)

    def scores_into(dst, left, right, h):
        for i in range(NBLK):
            rows = slice(i * BLK, (i + 1) * BLK)
            li = left[rows, cols(h)]
            for j in range(i + 1):
                s = mm(li, right[j * BLK:(j + 1) * BLK, cols(h)], NT)
                if i == j:
                    s = jnp.where(rows_i >= cols_i, s, 0.0)
                dst(rows, slice(j * BLK, (j + 1) * BLK), s.astype(BF16))

    def forward_unit(h):
        def put(rows, columns, val):
            sc[h, rows, columns] = val

        scores_into(put, q, k, h)
        for i in range(NBLK):
            rows = slice(i * BLK, (i + 1) * BLK)
            n = (i + 1) * BLK
            att[rows, cols(h)] = mm(sc[h, rows, 0:n], v[0:n, cols(h)], NN)

    def backward_unit(h):
        def put(rows, columns, val):
            dsb[rows, columns] = val

        scores_into(put, d, v, h)
        for i in range(NBLK):
            rows = slice(i * BLK, (i + 1) * BLK)
            n = (i + 1) * BLK
            g = mm(dsb[rows, 0:n], k[0:n, cols(h)], NN) + mm(d[rows, cols(h)], low[h], NT)
            gq[rows, cols(h)] = g.astype(BF16)
        qt = q[:, cols(h)].T
        dt = d[:, cols(h)].T
        for j in range(NBLK):
            columns = slice(j * BLK, (j + 1) * BLK)
            n = j * BLK
            gkp[columns, cols(h)] = mm(qt[:, n:], dsb[n:, columns], NN).T
            gvp[columns, cols(h)] = mm(dt[:, n:], sc[h, n:, columns], NN).T

    def all_to_all(src, dst, which):
        for o in others:
            send(src.at[o], dst.at[chip], fs_sem.at[which], fr_sem.at[which], dev(o, core, y)).start()
        dst[chip] = src[chip]

    def all_of(src, dst, which):
        n = CHIPS - 1
        return send(src.at[0:n], dst.at[0:n], fs_sem.at[which], fr_sem.at[which], partner)

    def scan(r, reverse, ready, term, start, work, done):
        swaps = []
        for ck in range(CHUNKS):
            ready(ck, 0)
            for i in range(PAIR):
                kv[r, 1, ck, i * (CHIPS // PAIR):(i + 1) * (CHIPS // PAIR)] = term(
                    head(1 - core, ck, i)
                ).reshape(CHIPS // PAIR, SL, DH)
            if r == 0 and ck == 0:
                pl.semaphore_wait(barrier, len(peers))
            swap = send(kv.at[r, 1, ck], cr.at[r, ck], cs_sem.at[r, 0, ck], cr_sem.at[r, 0, ck], partner)
            swap.start()
            swaps.append(swap)
            ready(ck, 1)
            for i in range(PAIR):
                kv[r, 0, ck, i * (CHIPS // PAIR):(i + 1) * (CHIPS // PAIR)] = term(
                    head(core, ck, i)
                ).reshape(CHIPS // PAIR, SL, DH)
            swap.wait_recv()
            cs[r, ck] = kv[r, 0, ck] + cr[r, ck]
            all_to_all(cs.at[r, ck], got.at[r, ck], (r, 0, ck))
        work(0)
        for ck in range(CHUNKS):
            all_of(cs.at[r, ck], got.at[r, ck], (r, 0, ck)).wait_recv()
            total = start(ck)
            for o in range(CHIPS - 1, -1, -1) if reverse else range(CHIPS):
                back[r, ck, o] = total
                total = total + got[r, ck, o]
            all_to_all(back.at[r, ck], pr.at[r, ck], (r, 1, ck))
            work(1 + ck)
        later = core == (0 if reverse else 1)
        for ck in range(CHUNKS):
            all_of(back.at[r, ck], pr.at[r, ck], (r, 1, ck)).wait_recv()
            fs[r, ck] = pr[r, ck] + jnp.where(later, 0.0, kv[r, 0, ck])
            swap = send(fs.at[r, ck], fr.at[r, ck], cs_sem.at[r, 1, ck], cr_sem.at[r, 1, ck], partner)
            swap.start()
            swaps.append(swap)
            for i in range(PAIR):
                part = slice(i * (CHIPS // PAIR), (i + 1) * (CHIPS // PAIR))
                val = pr[r, ck, part] + jnp.where(later, cr[r, ck, part], 0.0)
                done(head(core, ck, i), val.reshape(DH, DH))
            if ck == 0:
                work(3)
        for ck in range(CHUNKS):
            swaps[CHUNKS + ck].wait_recv()
            for i in range(PAIR):
                part = slice(i * (CHIPS // PAIR), (i + 1) * (CHIPS // PAIR))
                done(head(1 - core, ck, i), fr[r, ck, part].reshape(DH, DH))
        for swap in swaps:
            swap.wait_send()
        for ck in range(CHUNKS):
            all_of(cs.at[r, ck], got.at[r, ck], (r, 0, ck)).wait_send()
            all_of(back.at[r, ck], pr.at[r, ck], (r, 1, ck)).wait_send()

    def forward_ready(ck, side):
        loads["k", ck, side].wait()
        loads["v", ck, side].wait()

    def forward_term(h):
        return mm(k[:, cols(h)], v[:, cols(h)], TN)

    def forward_start(ck):
        loads["s", ck].wait()
        return s0[ck]

    def forward_work(n):
        if n == 0:
            loads["q"].wait()
            squares[...] = jnp.zeros_like(squares)
            cross[...] = jnp.zeros_like(cross)
        if n == 1:
            loads["c"].wait()
        loop(FORWARD_UNITS[n], FORWARD_UNITS[n + 1], forward_unit)

    def forward_done(h, val):
        state = val.astype(BF16)
        low[h] = state
        for i in range(NBLK):
            rows = slice(i * BLK, (i + 1) * BLK)
            a = att[rows, cols(h)] + mm(q[rows, cols(h)], state, NN)
            att[rows, cols(h)] = a
            squares[rows] += a * a
            cross[rows] += a * c[rows, cols(h)].astype(F32)

    scan(0, False, forward_ready, forward_term, forward_start, forward_work, forward_done)

    st[y] = jnp.zeros((8, TOK), F32)
    st[y, 0:1] = jnp.sum(squares[...].T, axis=0, keepdims=True)
    st[y, 1:2] = jnp.sum(cross[...].T, axis=0, keepdims=True)
    stats = [
        send(st.at[y], st.at[y], ys_sem.at[i - 1], yr_sem.at[i - 1], y_devs[i - 1]) for i in (2, 1, 3)
    ]
    for copy in stats:
        copy.start()
    for copy in stats:
        copy.wait()
    total = st[0] + st[1] + st[2] + st[3]
    inv = lax.rsqrt(total[0:1] / (HEADS * DH) + 1e-06)
    weight = inv * inv * inv * total[1:2] / (HEADS * DH)
    invb[...] = jnp.broadcast_to(inv, (DH, TOK)).T
    wb[...] = jnp.broadcast_to(weight, (DH, TOK)).T

    def backward_term(h):
        a = att[:, cols(h)]
        out[:, cols(h)] = (a * invb[...]).astype(BF16)
        dh = (invb[...] * c[:, cols(h)].astype(F32) - a * wb[...]).astype(BF16)
        d[:, cols(h)] = dh
        return mm(q[:, cols(h)], dh, TN)

    def backward_work(n):
        loop(BACKWARD_UNITS[n], BACKWARD_UNITS[n + 1], backward_unit)

    def backward_done(h, val):
        sfx[h] = val.astype(BF16)

    scan(
        1, True, lambda ck, side: None, backward_term, lambda ck: jnp.zeros((SL, DH), F32),
        backward_work, backward_done,
    )


def last_kernel(out_in, gq_in, gkp, gvp, k, v, sfx, out, gq, gk, gv, gkb, gvb, sem):
    first = [
        pltpu.make_async_copy(out_in, out, sem.at[0, 0]),
        pltpu.make_async_copy(gq_in, gq, sem.at[0, 1]),
    ]
    for copy in first:
        copy.start()
    later = []
    for h in range(HERE):
        hc = slice(h * DH, (h + 1) * DH)
        gkb[:, hc] = (gkp[:, hc] + mm(v[:, hc], sfx[h], NT)).astype(BF16)
        gvb[:, hc] = (gvp[:, hc] + mm(k[:, hc], sfx[h], NN)).astype(BF16)
        if h % 2 == 1:
            two = slice((h - 1) * DH, (h + 1) * DH)
            for n, (src, dst) in enumerate(((gkb, gk), (gvb, gv))):
                copy = pltpu.make_async_copy(src.at[:, two], dst.at[:, two], sem.at[1 + h // 2, n])
                copy.start()
                later.append(copy)
    for copy in first + later:
        copy.wait()


def local(*inputs):
    hbm = pl.BlockSpec(memory_space=pltpu.HBM)
    vmem = pl.BlockSpec(memory_space=pltpu.VMEM)
    wide = (TOK, FEAT)
    sums = (CHUNKS, CHIPS, SL, DH)
    mid = pl.pallas_call(
        main_kernel,
        name="scan_and_attention",
        out_shape=(
            pltpu.VMEM(wide, BF16),
            pltpu.VMEM(wide, BF16),
            pltpu.VMEM(wide, F32),
            pltpu.VMEM(wide, F32),
            pltpu.VMEM(wide, BF16),
            pltpu.VMEM(wide, BF16),
            pltpu.VMEM((HERE, DH, DH), BF16),
        ),
        in_specs=[hbm] * 5,
        out_specs=(vmem,) * 7,
        scratch_shapes=[
            pltpu.VMEM(wide, BF16),
            pltpu.VMEM(wide, BF16),
            pltpu.VMEM((CHUNKS, SL, DH), F32),
            pltpu.VMEM((HERE, TOK, TOK), BF16),
            pltpu.VMEM((TOK, TOK), BF16),
            pltpu.VMEM(wide, F32),
            pltpu.VMEM((TOK, DH), F32),
            pltpu.VMEM((TOK, DH), F32),
            pltpu.VMEM(wide, BF16),
            pltpu.VMEM((TOK, DH), F32),
            pltpu.VMEM((TOK, DH), F32),
            pltpu.VMEM((HERE, DH, DH), BF16),
            pltpu.VMEM((YS, 8, TOK), F32),
            pltpu.VMEM((2, 2) + sums, F32),
            pltpu.VMEM((2,) + sums, F32),
            pltpu.VMEM((2,) + sums, F32),
            pltpu.VMEM((2,) + sums, F32),
            pltpu.VMEM((2,) + sums, F32),
            pltpu.VMEM((2,) + sums, F32),
            pltpu.VMEM((2,) + sums, F32),
            pltpu.VMEM((2,) + sums, F32),
            pltpu.SemaphoreType.DMA((6 * CHUNKS + 2,)),
            pltpu.SemaphoreType.DMA((2, 2, CHUNKS)),
            pltpu.SemaphoreType.DMA((2, 2, CHUNKS)),
            pltpu.SemaphoreType.DMA((2, 2, CHUNKS)),
            pltpu.SemaphoreType.DMA((2, 2, CHUNKS)),
            pltpu.SemaphoreType.DMA((YS - 1,)),
            pltpu.SemaphoreType.DMA((YS - 1,)),
        ],
        compiler_params=pltpu.CompilerParams(
            collective_id=0, has_side_effects=True, vmem_limit_bytes=40 * 2**20
        ),
    )(*(pltpu.with_memory_space_constraint(a, pltpu.HBM) for a in inputs))
    return pl.pallas_call(
        last_kernel,
        name="add_states",
        out_shape=(jax.ShapeDtypeStruct(wide, BF16),) * 4,
        in_specs=[vmem] * 7,
        out_specs=(hbm,) * 4,
        scratch_shapes=[
            pltpu.VMEM(wide, BF16),
            pltpu.VMEM(wide, BF16),
            pltpu.SemaphoreType.DMA((5, 2)),
        ],
        compiler_params=pltpu.CompilerParams(vmem_limit_bytes=16 * 2**20),
    )(*mid)


def solution(mesh):
    wide = P("ctx", "head")
    return jax.shard_map(
        local,
        mesh=mesh,
        in_specs=(wide, wide, wide, wide, P("head", None, None)),
        out_specs=(wide, wide, wide, wide),
        check_vma=False,
    )
```

```python
import jax
import jax.numpy as jnp
from jax import lax
from jax.experimental import pallas as pl
from jax.experimental.pallas import tpu as pltpu
from jax.sharding import PartitionSpec as P

HEADS = 32
DH = 128
TOK = 768
HERE = 8
HALF = 4
FEAT = HERE * DH
XS, YS, ZS = 4, 4, 8
CHIPS = XS * ZS
CHUNKS = 2
PAIR = HALF // CHUNKS
SL = PAIR * DH // CHIPS
FAR_FIRST = sorted(
    ((dz, dx) for dz in (4, 3, 5, 2, 6, 1, 7, 0) for dx in (2, 1, 3, 0) if dz or dx),
    key=lambda p: (-min(p[0], ZS - p[0]) - min(p[1], XS - p[1]), 2 * p[0] > ZS),
)
FORWARD_UNITS = (0, 6, 7, 8, 8)
BACKWARD_UNITS = (0, 4, 5, 8, 8)
BLK = 256
NBLK = TOK // BLK
F32 = jnp.float32
BF16 = jnp.bfloat16

NN = (((1,), (0,)), ((), ()))
NT = (((1,), (1,)), ((), ()))
TN = (((0,), (0,)), ((), ()))


def mm(a, b, dims):
    return lax.dot_general(a, b, dims, preferred_element_type=F32)


def cols(h):
    return pl.ds(pl.multiple_of(h * DH, DH), DH)


def send(src, dst, ssem, rsem, target):
    return pltpu.make_async_remote_copy(
        src_ref=src,
        dst_ref=dst,
        send_sem=ssem,
        recv_sem=rsem,
        device_id=target,
        device_id_type=pl.DeviceIdType.MESH,
    )


def main_kernel(
    q_hbm, k_hbm, v_hbm, c_hbm, s_hbm,
    out, gq, gk, gv, gkp, gvp, k, v, sfx,
    q, c, s0, qt, sc, dsb, att, squares, cross, d, invb, wb, low, st,
    kv, cr, cs, got, back, pr, fs, fr,
    load_sem, cs_sem, cr_sem, fs_sem, fr_sem, ys_sem, yr_sem,
):
    ci = lax.axis_index("ctx")
    y = lax.axis_index("head")
    z = ci // (2 * XS)
    x = (ci // 2) % XS
    core = ci % 2
    chip = z * XS + x

    def dev(chip_index, cc, yy):
        return (chip_index * 2 + cc, yy)

    partner = dev(chip, 1 - core, y)
    others = [((z + dz) % ZS) * XS + (x + dx) % XS for dz, dx in FAR_FIRST]
    y_devs = [dev(chip, core, (y + i) % YS) for i in range(1, YS)]
    peers = [dev(o, core, y) for o in others] + y_devs + [partner]

    barrier = pltpu.get_barrier_semaphore()
    for peer in peers:
        pl.semaphore_signal(barrier, inc=1, device_id=peer, device_id_type=pl.DeviceIdType.MESH)

    def head(half, ck, i=0):
        return half * HALF + ck * PAIR + i

    def pair_cols(half, ck):
        return pl.ds(pl.multiple_of(head(half, ck) * DH, PAIR * DH), PAIR * DH)

    loads = {}

    def load(name, src, dst):
        copy = pltpu.make_async_copy(src, dst, load_sem.at[len(loads)])
        copy.start()
        loads[name] = copy

    for side, half in enumerate((1 - core, core)):
        for ck in range(CHUNKS):
            part = pair_cols(half, ck)
            load(("k", ck, side), k_hbm.at[:, part], k.at[:, part])
            load(("v", ck, side), v_hbm.at[:, part], v.at[:, part])
    load("q", q_hbm, q)
    for ck in range(CHUNKS):
        rows = pl.ds(pl.multiple_of((chip % (CHIPS // PAIR)) * SL, SL), SL)
        load(("s", ck), s_hbm.at[head(core, ck) + chip // (CHIPS // PAIR), rows], s0.at[ck])
    load("c", c_hbm, c)

    def loop(lo, hi, body):
        def step(i, carry):
            body(i)
            return carry

        if hi > lo:
            lax.fori_loop(lo, hi, step, 0)

    rows_i = lax.broadcasted_iota(jnp.int32, (BLK, BLK), 0)
    cols_i = lax.broadcasted_iota(jnp.int32, (BLK, BLK), 1)

    def scores_into(dst, left, right, h):
        for i in range(NBLK):
            rows = slice(i * BLK, (i + 1) * BLK)
            li = left[rows, cols(h)]
            for j in range(i + 1):
                s = mm(li, right[j * BLK:(j + 1) * BLK, cols(h)], NT)
                if i == j:
                    s = jnp.where(rows_i >= cols_i, s, 0.0)
                dst(rows, slice(j * BLK, (j + 1) * BLK), s.astype(BF16))

    def forward_unit(h):
        def put(rows, columns, val):
            sc[h, rows, columns] = val

        qt[h] = q[:, cols(h)].T
        scores_into(put, q, k, h)
        for i in range(NBLK):
            rows = slice(i * BLK, (i + 1) * BLK)
            n = (i + 1) * BLK
            att[rows, cols(h)] = mm(sc[h, rows, 0:n], v[0:n, cols(h)], NN)

    def backward_unit(h):
        def put(rows, columns, val):
            dsb[rows, columns] = val

        out[:, cols(h)] = (att[:, cols(h)] * invb[...]).astype(BF16)
        scores_into(put, d, v, h)
        for i in range(NBLK):
            rows = slice(i * BLK, (i + 1) * BLK)
            n = (i + 1) * BLK
            g = mm(dsb[rows, 0:n], k[0:n, cols(h)], NN) + mm(d[rows, cols(h)], low[h], NT)
            gq[rows, cols(h)] = g.astype(BF16)
        dt = d[:, cols(h)].T
        for j in range(NBLK):
            columns = slice(j * BLK, (j + 1) * BLK)
            n = j * BLK
            gkp[columns, cols(h)] = mm(qt[h, :, n:], dsb[n:, columns], NN).T
            gvp[columns, cols(h)] = mm(dt[:, n:], sc[h, n:, columns], NN).T

    def all_to_all(src, dst, which):
        for o in others:
            send(src.at[o], dst.at[chip], fs_sem.at[which], fr_sem.at[which], dev(o, core, y)).start()
        dst[chip] = src[chip]

    def all_of(src, dst, which):
        n = CHIPS - 1
        return send(src.at[0:n], dst.at[0:n], fs_sem.at[which], fr_sem.at[which], partner)

    def scan(r, reverse, ready, term, start, work, done):
        def terms(side, half, ck):
            for i in range(PAIR):
                part = slice(i * (CHIPS // PAIR), (i + 1) * (CHIPS // PAIR))
                kv[r, side, ck, part] = term(head(half, ck, i)).reshape(CHIPS // PAIR, SL, DH)

        swaps = []
        for ck in range(CHUNKS):
            ready(ck, 0)
            terms(1, 1 - core, ck)
            if r == 0 and ck == 0:
                pl.semaphore_wait(barrier, len(peers))
            swap = send(kv.at[r, 1, ck], cr.at[r, ck], cs_sem.at[r, 0, ck], cr_sem.at[r, 0, ck], partner)
            swap.start()
            swaps.append(swap)
        for ck in range(CHUNKS):
            ready(ck, 1)
            terms(0, core, ck)
            swaps[ck].wait_recv()
            cs[r, ck] = kv[r, 0, ck] + cr[r, ck]
            all_to_all(cs.at[r, ck], got.at[r, ck], (r, 0, ck))
        work(0)
        for ck in range(CHUNKS):
            all_of(cs.at[r, ck], got.at[r, ck], (r, 0, ck)).wait_recv()
            total = start(ck)
            for o in range(CHIPS - 1, -1, -1) if reverse else range(CHIPS):
                back[r, ck, o] = total
                total = total + got[r, ck, o]
            all_to_all(back.at[r, ck], pr.at[r, ck], (r, 1, ck))
            work(1 + ck)
        later = core == (0 if reverse else 1)
        for ck in range(CHUNKS):
            all_of(back.at[r, ck], pr.at[r, ck], (r, 1, ck)).wait_recv()
            fs[r, ck] = pr[r, ck] + jnp.where(later, 0.0, kv[r, 0, ck])
            swap = send(fs.at[r, ck], fr.at[r, ck], cs_sem.at[r, 1, ck], cr_sem.at[r, 1, ck], partner)
            swap.start()
            swaps.append(swap)
            parts = [slice(i * (CHIPS // PAIR), (i + 1) * (CHIPS // PAIR)) for i in range(PAIR)]
            for i, part in enumerate(parts):
                val = pr[r, ck, part] + jnp.where(later, cr[r, ck, part], 0.0)
                done(head(core, ck, i), val.reshape(DH, DH), False)
            if ck == 0:
                work(3)
            swap.wait_recv()
            for i, part in enumerate(parts):
                done(head(1 - core, ck, i), fr[r, ck, part].reshape(DH, DH), ck == CHUNKS - 1)
        for swap in swaps:
            swap.wait_send()
        for ck in range(CHUNKS):
            all_of(cs.at[r, ck], got.at[r, ck], (r, 0, ck)).wait_send()
            all_of(back.at[r, ck], pr.at[r, ck], (r, 1, ck)).wait_send()

    def forward_ready(ck, side):
        loads["k", ck, side].wait()
        loads["v", ck, side].wait()

    def forward_term(h):
        return mm(k[:, cols(h)], v[:, cols(h)], TN)

    def forward_start(ck):
        loads["s", ck].wait()
        return s0[ck]

    def forward_work(n):
        if n == 0:
            loads["q"].wait()
            squares[...] = jnp.zeros_like(squares)
            cross[...] = jnp.zeros_like(cross)
        if n == 1:
            loads["c"].wait()
        loop(FORWARD_UNITS[n], FORWARD_UNITS[n + 1], forward_unit)

    def forward_done(h, val, last):
        state = val.astype(BF16)
        low[h] = state
        for i in range(NBLK):
            rows = slice(i * BLK, (i + 1) * BLK)
            a = att[rows, cols(h)] + mm(q[rows, cols(h)], state, NN)
            att[rows, cols(h)] = a
            squares[rows] += a * a
            cross[rows] += a * c[rows, cols(h)].astype(F32)

    scan(0, False, forward_ready, forward_term, forward_start, forward_work, forward_done)

    st[y, 0:1] = jnp.sum(squares[...].T, axis=0, keepdims=True)
    st[y, 1:2] = jnp.sum(cross[...].T, axis=0, keepdims=True)
    stats = [
        send(st.at[y], st.at[y], ys_sem.at[i - 1], yr_sem.at[i - 1], y_devs[i - 1]) for i in (2, 1, 3)
    ]
    for copy in stats:
        copy.start()
    for copy in stats:
        copy.wait_recv()
    total = st[0] + st[1] + st[2] + st[3]
    inv = lax.rsqrt(total[0:1] / (HEADS * DH) + 1e-06)
    weight = inv * inv * inv * total[1:2] / (HEADS * DH)
    invb[...] = jnp.broadcast_to(inv, (DH, TOK)).T
    wb[...] = jnp.broadcast_to(weight, (DH, TOK)).T

    def backward_term(h):
        a = att[:, cols(h)]
        dh = (invb[...] * c[:, cols(h)].astype(F32) - a * wb[...]).astype(BF16)
        d[:, cols(h)] = dh
        return mm(qt[h], dh, NN)

    def backward_work(n):
        loop(BACKWARD_UNITS[n], BACKWARD_UNITS[n + 1], backward_unit)

    def backward_done(h, val, last):
        state = val.astype(BF16)
        if last:
            sfx[h] = state
        else:
            gk[:, cols(h)] = (gkp[:, cols(h)] + mm(v[:, cols(h)], state, NT)).astype(BF16)
            gv[:, cols(h)] = (gvp[:, cols(h)] + mm(k[:, cols(h)], state, NN)).astype(BF16)

    scan(
        1, True, lambda ck, side: None, backward_term, lambda ck: jnp.zeros((SL, DH), F32),
        backward_work, backward_done,
    )
    for copy in stats:
        copy.wait_send()


def last_kernel(out_in, gq_in, gk_in, gv_in, gkp, gvp, k, v, sfx, out, gq, gk, gv, gkb, gvb, sem):
    core = lax.axis_index("ctx") % 2
    own = pl.ds(pl.multiple_of(core * HALF * DH, HALF * DH), HALF * DH)
    head = (1 - core) * HALF
    early = pl.ds(pl.multiple_of(head * DH, PAIR * DH), PAIR * DH)
    late = pl.ds(pl.multiple_of((head + PAIR) * DH, PAIR * DH), PAIR * DH)
    copies = []

    def copy(src, dst):
        copies.append(pltpu.make_async_copy(src, dst, sem.at[len(copies)]))
        copies[-1].start()

    copy(out_in, out)
    copy(gq_in, gq)
    for part in (own, early):
        copy(gk_in.at[:, part], gk.at[:, part])
        copy(gv_in.at[:, part], gv.at[:, part])
    for i in range(PAIR):
        h = head + PAIR + i
        here = slice(i * DH, (i + 1) * DH)
        gkb[:, here] = (gkp[:, cols(h)] + mm(v[:, cols(h)], sfx[h], NT)).astype(BF16)
        gvb[:, here] = (gvp[:, cols(h)] + mm(k[:, cols(h)], sfx[h], NN)).astype(BF16)
    copy(gkb, gk.at[:, late])
    copy(gvb, gv.at[:, late])
    for c in copies:
        c.wait()


def local(*inputs):
    hbm = pl.BlockSpec(memory_space=pltpu.HBM)
    vmem = pl.BlockSpec(memory_space=pltpu.VMEM)
    wide = (TOK, FEAT)
    sums = (CHUNKS, CHIPS, SL, DH)
    mid = pl.pallas_call(
        main_kernel,
        name="scan_and_attention",
        out_shape=(
            pltpu.VMEM(wide, BF16),
            pltpu.VMEM(wide, BF16),
            pltpu.VMEM(wide, BF16),
            pltpu.VMEM(wide, BF16),
            pltpu.VMEM(wide, F32),
            pltpu.VMEM(wide, F32),
            pltpu.VMEM(wide, BF16),
            pltpu.VMEM(wide, BF16),
            pltpu.VMEM((HERE, DH, DH), BF16),
        ),
        in_specs=[hbm] * 5,
        out_specs=(vmem,) * 9,
        scratch_shapes=[
            pltpu.VMEM(wide, BF16),
            pltpu.VMEM(wide, BF16),
            pltpu.VMEM((CHUNKS, SL, DH), F32),
            pltpu.VMEM((HERE, DH, TOK), BF16),
            pltpu.VMEM((HERE, TOK, TOK), BF16),
            pltpu.VMEM((TOK, TOK), BF16),
            pltpu.VMEM(wide, F32),
            pltpu.VMEM((TOK, DH), F32),
            pltpu.VMEM((TOK, DH), F32),
            pltpu.VMEM(wide, BF16),
            pltpu.VMEM((TOK, DH), F32),
            pltpu.VMEM((TOK, DH), F32),
            pltpu.VMEM((HERE, DH, DH), BF16),
            pltpu.VMEM((YS, 2, TOK), F32),
            pltpu.VMEM((2, 2) + sums, F32),
            pltpu.VMEM((2,) + sums, F32),
            pltpu.VMEM((2,) + sums, F32),
            pltpu.VMEM((2,) + sums, F32),
            pltpu.VMEM((2,) + sums, F32),
            pltpu.VMEM((2,) + sums, F32),
            pltpu.VMEM((2,) + sums, F32),
            pltpu.VMEM((2,) + sums, F32),
            pltpu.SemaphoreType.DMA((6 * CHUNKS + 2,)),
            pltpu.SemaphoreType.DMA((2, 2, CHUNKS)),
            pltpu.SemaphoreType.DMA((2, 2, CHUNKS)),
            pltpu.SemaphoreType.DMA((2, 2, CHUNKS)),
            pltpu.SemaphoreType.DMA((2, 2, CHUNKS)),
            pltpu.SemaphoreType.DMA((YS - 1,)),
            pltpu.SemaphoreType.DMA((YS - 1,)),
        ],
        compiler_params=pltpu.CompilerParams(
            collective_id=0, has_side_effects=True, vmem_limit_bytes=40 * 2**20
        ),
    )(*(pltpu.with_memory_space_constraint(a, pltpu.HBM) for a in inputs))
    return pl.pallas_call(
        last_kernel,
        name="add_states",
        out_shape=(jax.ShapeDtypeStruct(wide, BF16),) * 4,
        in_specs=[vmem] * 9,
        out_specs=(hbm,) * 4,
        scratch_shapes=[
            pltpu.VMEM((TOK, PAIR * DH), BF16),
            pltpu.VMEM((TOK, PAIR * DH), BF16),
            pltpu.SemaphoreType.DMA((8,)),
        ],
        compiler_params=pltpu.CompilerParams(vmem_limit_bytes=16 * 2**20),
    )(*mid)


def solution(mesh):
    wide = P("ctx", "head")
    return jax.shard_map(
        local,
        mesh=mesh,
        in_specs=(wide, wide, wide, wide, P("head", None, None)),
        out_specs=(wide, wide, wide, wide),
        check_vma=False,
    )
```

```python
import jax
import jax.numpy as jnp
from jax import lax
from jax.experimental import pallas as pl
from jax.experimental.pallas import tpu as pltpu
from jax.sharding import PartitionSpec as P

HEADS = 32
DH = 128
TOK = 768
HERE = 8
HALF = 4
FEAT = HERE * DH
XS, YS, ZS = 4, 4, 8
CHIPS = XS * ZS
CHUNKS = 2
PAIR = HALF // CHUNKS
SL = PAIR * DH // CHIPS
FAR_FIRST = sorted(
    ((dz, dx) for dz in (4, 3, 5, 2, 6, 1, 7, 0) for dx in (2, 1, 3, 0) if dz or dx),
    key=lambda p: (-min(p[0], ZS - p[0]) - min(p[1], XS - p[1]), 2 * p[0] > ZS),
)
FORWARD_UNITS = (0, 6, 7, 8, 8)
BACKWARD_UNITS = (0, 4, 5, 8, 8)
BLK = 256
NBLK = TOK // BLK
F32 = jnp.float32
BF16 = jnp.bfloat16

NN = (((1,), (0,)), ((), ()))
NT = (((1,), (1,)), ((), ()))
TN = (((0,), (0,)), ((), ()))


def mm(a, b, dims):
    return lax.dot_general(a, b, dims, preferred_element_type=F32)


def cols(h):
    return pl.ds(pl.multiple_of(h * DH, DH), DH)


def send(src, dst, ssem, rsem, target):
    return pltpu.make_async_remote_copy(
        src_ref=src,
        dst_ref=dst,
        send_sem=ssem,
        recv_sem=rsem,
        device_id=target,
        device_id_type=pl.DeviceIdType.MESH,
    )


def main_kernel(
    q_hbm, k_hbm, v_hbm, c_hbm, s_hbm,
    out, gq, gk, gv, gkp, gvp, k, v, sfx,
    q, c, s0, qt, sc, dsb, att, squares, cross, d, invb, wb, low, st,
    kv, cr, cs, got, back, pr, fs, fr,
    load_sem, cs_sem, cr_sem, fs_sem, fr_sem, ys_sem, yr_sem,
):
    ci = lax.axis_index("ctx")
    y = lax.axis_index("head")
    z = ci // (2 * XS)
    x = (ci // 2) % XS
    core = ci % 2
    chip = z * XS + x

    def dev(chip_index, cc, yy):
        return (chip_index * 2 + cc, yy)

    partner = dev(chip, 1 - core, y)
    others = [((z + dz) % ZS) * XS + (x + dx) % XS for dz, dx in FAR_FIRST]
    y_devs = [dev(chip, core, (y + i) % YS) for i in range(1, YS)]
    peers = [dev(o, core, y) for o in others] + y_devs + [partner]

    barrier = pltpu.get_barrier_semaphore()
    for peer in peers:
        pl.semaphore_signal(barrier, inc=1, device_id=peer, device_id_type=pl.DeviceIdType.MESH)

    def head(half, ck, i=0):
        return half * HALF + ck * PAIR + i

    def pair_cols(half, ck):
        return pl.ds(pl.multiple_of(head(half, ck) * DH, PAIR * DH), PAIR * DH)

    loads = {}

    def load(name, src, dst):
        copy = pltpu.make_async_copy(src, dst, load_sem.at[len(loads)])
        copy.start()
        loads[name] = copy

    for side, half in enumerate((1 - core, core)):
        for ck in range(CHUNKS):
            part = pair_cols(half, ck)
            load(("k", ck, side), k_hbm.at[:, part], k.at[:, part])
            load(("v", ck, side), v_hbm.at[:, part], v.at[:, part])
    load("q", q_hbm, q)
    for ck in range(CHUNKS):
        rows = pl.ds(pl.multiple_of((chip % (CHIPS // PAIR)) * SL, SL), SL)
        load(("s", ck), s_hbm.at[head(core, ck) + chip // (CHIPS // PAIR), rows], s0.at[ck])
    load("c", c_hbm, c)

    def loop(lo, hi, body):
        def step(i, carry):
            body(i)
            return carry

        if hi > lo:
            lax.fori_loop(lo, hi, step, 0)

    rows_i = lax.broadcasted_iota(jnp.int32, (BLK, BLK), 0)
    cols_i = lax.broadcasted_iota(jnp.int32, (BLK, BLK), 1)

    def scores_into(dst, left, right, h):
        for i in range(NBLK):
            rows = slice(i * BLK, (i + 1) * BLK)
            li = left[rows, cols(h)]
            for j in range(i + 1):
                s = mm(li, right[j * BLK:(j + 1) * BLK, cols(h)], NT)
                if i == j:
                    s = jnp.where(rows_i >= cols_i, s, 0.0)
                dst(rows, slice(j * BLK, (j + 1) * BLK), s.astype(BF16))

    def forward_unit(h):
        def put(rows, columns, val):
            sc[h, rows, columns] = val

        qt[h] = q[:, cols(h)].T
        scores_into(put, q, k, h)
        for i in range(NBLK):
            rows = slice(i * BLK, (i + 1) * BLK)
            n = (i + 1) * BLK
            att[rows, cols(h)] = mm(sc[h, rows, 0:n], v[0:n, cols(h)], NN)

    def backward_unit(h):
        def put(rows, columns, val):
            dsb[rows, columns] = val

        out[:, cols(h)] = (att[:, cols(h)] * invb[...]).astype(BF16)
        scores_into(put, d, v, h)
        for i in range(NBLK):
            rows = slice(i * BLK, (i + 1) * BLK)
            n = (i + 1) * BLK
            g = mm(dsb[rows, 0:n], k[0:n, cols(h)], NN) + mm(d[rows, cols(h)], low[h], NT)
            gq[rows, cols(h)] = g.astype(BF16)
        dt = d[:, cols(h)].T
        for j in range(NBLK):
            columns = slice(j * BLK, (j + 1) * BLK)
            n = j * BLK
            gkp[columns, cols(h)] = mm(qt[h, :, n:], dsb[n:, columns], NN).T
            gvp[columns, cols(h)] = mm(dt[:, n:], sc[h, n:, columns], NN).T

    def all_to_all(src, dst, which):
        for o in others:
            send(src.at[o], dst.at[chip], fs_sem.at[which], fr_sem.at[which], dev(o, core, y)).start()
        dst[chip] = src[chip]

    def all_of(src, dst, which):
        n = CHIPS - 1
        return send(src.at[0:n], dst.at[0:n], fs_sem.at[which], fr_sem.at[which], partner)

    def scan(r, reverse, ready, term, start, work, done):
        def terms(side, half, ck):
            for i in range(PAIR):
                part = slice(i * (CHIPS // PAIR), (i + 1) * (CHIPS // PAIR))
                kv[r, side, ck, part] = term(head(half, ck, i)).reshape(CHIPS // PAIR, SL, DH)

        swaps = []

        def first(ck):
            ready(ck, 0)
            terms(1, 1 - core, ck)
            if r == 0 and ck == 0:
                pl.semaphore_wait(barrier, len(peers))
            swap = send(kv.at[r, 1, ck], cr.at[r, ck], cs_sem.at[r, 0, ck], cr_sem.at[r, 0, ck], partner)
            swap.start()
            swaps.append(swap)

        def second(ck):
            ready(ck, 1)
            terms(0, core, ck)
            swaps[ck].wait_recv()
            cs[r, ck] = kv[r, 0, ck] + cr[r, ck]
            all_to_all(cs.at[r, ck], got.at[r, ck], (r, 0, ck))

        if r == 0:
            first(0), first(1), second(0), second(1)
        else:
            first(0), second(0), first(1), second(1)
        work(0)
        for ck in range(CHUNKS):
            all_of(cs.at[r, ck], got.at[r, ck], (r, 0, ck)).wait_recv()
            total = start(ck)
            for o in range(CHIPS - 1, -1, -1) if reverse else range(CHIPS):
                back[r, ck, o] = total
                total = total + got[r, ck, o]
            all_to_all(back.at[r, ck], pr.at[r, ck], (r, 1, ck))
            work(1 + ck)
        later = core == (0 if reverse else 1)
        for ck in range(CHUNKS):
            all_of(back.at[r, ck], pr.at[r, ck], (r, 1, ck)).wait_recv()
            fs[r, ck] = pr[r, ck] + jnp.where(later, 0.0, kv[r, 0, ck])
            swap = send(fs.at[r, ck], fr.at[r, ck], cs_sem.at[r, 1, ck], cr_sem.at[r, 1, ck], partner)
            swap.start()
            swaps.append(swap)
            parts = [slice(i * (CHIPS // PAIR), (i + 1) * (CHIPS // PAIR)) for i in range(PAIR)]
            for i, part in enumerate(parts):
                val = pr[r, ck, part] + jnp.where(later, cr[r, ck, part], 0.0)
                done(head(core, ck, i), val.reshape(DH, DH), False)
            if ck == 0:
                work(3)
            swap.wait_recv()
            for i, part in enumerate(parts):
                done(head(1 - core, ck, i), fr[r, ck, part].reshape(DH, DH), ck == CHUNKS - 1)
        for swap in swaps:
            swap.wait_send()
        for ck in range(CHUNKS):
            all_of(cs.at[r, ck], got.at[r, ck], (r, 0, ck)).wait_send()
            all_of(back.at[r, ck], pr.at[r, ck], (r, 1, ck)).wait_send()

    def forward_ready(ck, side):
        loads["k", ck, side].wait()
        loads["v", ck, side].wait()

    def forward_term(h):
        return mm(k[:, cols(h)], v[:, cols(h)], TN)

    def forward_start(ck):
        loads["s", ck].wait()
        return s0[ck]

    def forward_work(n):
        if n == 0:
            loads["q"].wait()
            squares[...] = jnp.zeros_like(squares)
            cross[...] = jnp.zeros_like(cross)
        if n == 1:
            loads["c"].wait()
        loop(FORWARD_UNITS[n], FORWARD_UNITS[n + 1], forward_unit)

    def forward_done(h, val, last):
        state = val.astype(BF16)
        low[h] = state
        for i in range(NBLK):
            rows = slice(i * BLK, (i + 1) * BLK)
            a = att[rows, cols(h)] + mm(q[rows, cols(h)], state, NN)
            att[rows, cols(h)] = a
            squares[rows] += a * a
            cross[rows] += a * c[rows, cols(h)].astype(F32)

    scan(0, False, forward_ready, forward_term, forward_start, forward_work, forward_done)

    st[y, 0:1] = jnp.sum(squares[...].T, axis=0, keepdims=True)
    st[y, 1:2] = jnp.sum(cross[...].T, axis=0, keepdims=True)
    stats = [
        send(st.at[y], st.at[y], ys_sem.at[i - 1], yr_sem.at[i - 1], y_devs[i - 1]) for i in (2, 1, 3)
    ]
    for copy in stats:
        copy.start()
    for copy in stats:
        copy.wait_recv()
    total = st[0] + st[1] + st[2] + st[3]
    inv = lax.rsqrt(total[0:1] / (HEADS * DH) + 1e-06)
    weight = inv * inv * inv * total[1:2] / (HEADS * DH)
    invb[...] = jnp.broadcast_to(inv, (DH, TOK)).T
    wb[...] = jnp.broadcast_to(weight, (DH, TOK)).T

    def backward_term(h):
        a = att[:, cols(h)]
        dh = (invb[...] * c[:, cols(h)].astype(F32) - a * wb[...]).astype(BF16)
        d[:, cols(h)] = dh
        return mm(qt[h], dh, NN)

    def backward_work(n):
        loop(BACKWARD_UNITS[n], BACKWARD_UNITS[n + 1], backward_unit)

    def backward_done(h, val, last):
        state = val.astype(BF16)
        if last:
            sfx[h] = state
        else:
            gk[:, cols(h)] = (gkp[:, cols(h)] + mm(v[:, cols(h)], state, NT)).astype(BF16)
            gv[:, cols(h)] = (gvp[:, cols(h)] + mm(k[:, cols(h)], state, NN)).astype(BF16)

    scan(
        1, True, lambda ck, side: None, backward_term, lambda ck: jnp.zeros((SL, DH), F32),
        backward_work, backward_done,
    )
    for copy in stats:
        copy.wait_send()


def last_kernel(out_in, gq_in, gk_in, gv_in, gkp, gvp, k, v, sfx, out, gq, gk, gv, gkb, gvb, sem):
    core = lax.axis_index("ctx") % 2
    own = pl.ds(pl.multiple_of(core * HALF * DH, HALF * DH), HALF * DH)
    head = (1 - core) * HALF
    early = pl.ds(pl.multiple_of(head * DH, PAIR * DH), PAIR * DH)
    late = pl.ds(pl.multiple_of((head + PAIR) * DH, PAIR * DH), PAIR * DH)
    copies = []

    def copy(src, dst):
        copies.append(pltpu.make_async_copy(src, dst, sem.at[len(copies)]))
        copies[-1].start()

    copy(out_in, out)
    copy(gq_in, gq)
    for part in (own, early):
        copy(gk_in.at[:, part], gk.at[:, part])
        copy(gv_in.at[:, part], gv.at[:, part])
    for i in range(PAIR):
        h = head + PAIR + i
        here = slice(i * DH, (i + 1) * DH)
        gkb[:, here] = (gkp[:, cols(h)] + mm(v[:, cols(h)], sfx[h], NT)).astype(BF16)
        gvb[:, here] = (gvp[:, cols(h)] + mm(k[:, cols(h)], sfx[h], NN)).astype(BF16)
    copy(gkb, gk.at[:, late])
    copy(gvb, gv.at[:, late])
    for c in copies:
        c.wait()


def local(*inputs):
    hbm = pl.BlockSpec(memory_space=pltpu.HBM)
    vmem = pl.BlockSpec(memory_space=pltpu.VMEM)
    wide = (TOK, FEAT)
    sums = (CHUNKS, CHIPS, SL, DH)
    mid = pl.pallas_call(
        main_kernel,
        name="scan_and_attention",
        out_shape=(
            pltpu.VMEM(wide, BF16),
            pltpu.VMEM(wide, BF16),
            pltpu.VMEM(wide, BF16),
            pltpu.VMEM(wide, BF16),
            pltpu.VMEM(wide, F32),
            pltpu.VMEM(wide, F32),
            pltpu.VMEM(wide, BF16),
            pltpu.VMEM(wide, BF16),
            pltpu.VMEM((HERE, DH, DH), BF16),
        ),
        in_specs=[hbm] * 5,
        out_specs=(vmem,) * 9,
        scratch_shapes=[
            pltpu.VMEM(wide, BF16),
            pltpu.VMEM(wide, BF16),
            pltpu.VMEM((CHUNKS, SL, DH), F32),
            pltpu.VMEM((HERE, DH, TOK), BF16),
            pltpu.VMEM((HERE, TOK, TOK), BF16),
            pltpu.VMEM((TOK, TOK), BF16),
            pltpu.VMEM(wide, F32),
            pltpu.VMEM((TOK, DH), F32),
            pltpu.VMEM((TOK, DH), F32),
            pltpu.VMEM(wide, BF16),
            pltpu.VMEM((TOK, DH), F32),
            pltpu.VMEM((TOK, DH), F32),
            pltpu.VMEM((HERE, DH, DH), BF16),
            pltpu.VMEM((YS, 2, TOK), F32),
            pltpu.VMEM((2, 2) + sums, F32),
            pltpu.VMEM((2,) + sums, F32),
            pltpu.VMEM((2,) + sums, F32),
            pltpu.VMEM((2,) + sums, F32),
            pltpu.VMEM((2,) + sums, F32),
            pltpu.VMEM((2,) + sums, F32),
            pltpu.VMEM((2,) + sums, F32),
            pltpu.VMEM((2,) + sums, F32),
            pltpu.SemaphoreType.DMA((6 * CHUNKS + 2,)),
            pltpu.SemaphoreType.DMA((2, 2, CHUNKS)),
            pltpu.SemaphoreType.DMA((2, 2, CHUNKS)),
            pltpu.SemaphoreType.DMA((2, 2, CHUNKS)),
            pltpu.SemaphoreType.DMA((2, 2, CHUNKS)),
            pltpu.SemaphoreType.DMA((YS - 1,)),
            pltpu.SemaphoreType.DMA((YS - 1,)),
        ],
        compiler_params=pltpu.CompilerParams(
            collective_id=0, has_side_effects=True, vmem_limit_bytes=40 * 2**20
        ),
    )(*(pltpu.with_memory_space_constraint(a, pltpu.HBM) for a in inputs))
    return pl.pallas_call(
        last_kernel,
        name="add_states",
        out_shape=(jax.ShapeDtypeStruct(wide, BF16),) * 4,
        in_specs=[vmem] * 9,
        out_specs=(hbm,) * 4,
        scratch_shapes=[
            pltpu.VMEM((TOK, PAIR * DH), BF16),
            pltpu.VMEM((TOK, PAIR * DH), BF16),
            pltpu.SemaphoreType.DMA((8,)),
        ],
        compiler_params=pltpu.CompilerParams(vmem_limit_bytes=16 * 2**20),
    )(*mid)


def solution(mesh):
    wide = P("ctx", "head")
    return jax.shard_map(
        local,
        mesh=mesh,
        in_specs=(wide, wide, wide, wide, P("head", None, None)),
        out_specs=(wide, wide, wide, wide),
        check_vma=False,
    )
```
